32 devices in a mesh: groups: 2 (over y), seq: 4 (over z), head: 2 (over x), batch: 2 (over core).
Axes of the slice: x: 2, y: 2, z: 4, core: 2. Of those that a mesh axis runs over, the one named last changes fastest.
Arguments:
- queries: bfloat16 [4, 2048, 256], P(('groups', 'batch'), 'seq', 'head'), parts along dimension 0, may hold values from -8 to 8
- key_vectors: bfloat16 [4, 2048, 256], P(('groups', 'batch'), 'seq', 'head'), parts along dimension 0, may hold values from -8 to 8
- value_vectors: bfloat16 [4, 2048, 2048], P(('groups', 'batch'), 'seq', 'head'), parts along dimension 0, may hold values from -6 to 6
Outputs:
- mixture: bfloat16 [4, 2048, 2048], P(('groups', 'batch'), 'seq', 'head'), parts along dimension 0
The draws below stay inside these ranges and needn't reach their ends.
There are 2 independent parts, one for each index of `groups`. The reference program is written for one: setup_inputs(seed, part) draws one part's arguments, and reference() takes and returns one part's arrays. A program takes and returns all parts, laid end to end along the dimension named above; each array names one. Nothing has to cross between parts.
All inputs are finite; a program needn't handle non-finite values.
Results may differ from the reference program's by a relative error of at most 0.0034.
Values may be sent and summed in bfloat16 or wider, within the bound.
A program may use at most 64 MiB of HBM per device.

```python
import math
import jax
import jax.numpy as jnp
import numpy as np
from jax import lax

HEADS = 16
DK = 16
DV = 128
WINDOW = 64
T_DEV = 512
FEAT = 153
LENGTH = 2048
BATCH = 2


def drawn_pair(key):
    shape = (BATCH, LENGTH, HEADS, DK)
    base_queries = jnp.clip(jax.random.normal(jax.random.fold_in(key, 11), shape, jnp.float32), -6.0, 6.0)
    base_keys = jnp.clip(jax.random.normal(jax.random.fold_in(key, 12), shape, jnp.float32), -6.0, 6.0)
    return (base_queries.reshape(BATCH, LENGTH, HEADS * DK), base_keys.reshape(BATCH, LENGTH, HEADS * DK))


def draw_queries(key, part):
    return drawn_pair(key)[0].astype(jnp.bfloat16)


def draw_key_vectors(key, part):
    return drawn_pair(key)[1].astype(jnp.bfloat16)


def draw_value_vectors(key, part):
    shape = (BATCH, LENGTH, HEADS * DV)
    regions = jax.random.uniform(jax.random.fold_in(key, 21), (BATCH, 32, HEADS * DV), jnp.float32, -1.5, 1.5)
    noise = jax.random.normal(jax.random.fold_in(key, 22), shape, jnp.float32)
    offsets = jnp.repeat(regions, LENGTH // 32, axis=1)
    return jnp.clip(noise + offsets, -6.0, 6.0).astype(jnp.bfloat16)


def setup_inputs(seed: int = 0, part: int = 0) -> dict:
    arg_keys = jax.random.split(jax.random.key(seed), 4)
    part_keys = jax.random.split(jax.random.fold_in(arg_keys[3], part), 4)
    return {
        "queries": draw_queries(jax.random.fold_in(jax.random.fold_in(arg_keys[3], part), 71), part),
        "key_vectors": draw_key_vectors(jax.random.fold_in(jax.random.fold_in(arg_keys[3], part), 71), part),
        "value_vectors": draw_value_vectors(jax.random.fold_in(jax.random.fold_in(arg_keys[3], part), 71), part),
    }


def features(vectors):
    upper_rows, upper_cols = np.triu_indices(DK)
    pair_weights = np.where(upper_rows == upper_cols, 1.0 / math.sqrt(2.0 * DK), 1.0 / math.sqrt(DK))
    paired = vectors[:, upper_rows] * vectors[:, upper_cols] * jnp.asarray(pair_weights, dtype=vectors.dtype)
    leading = jnp.ones((vectors.shape[0], 1), vectors.dtype)
    return jnp.concatenate([leading, vectors * DK ** (-0.25), paired], axis=1)

def block_state(key_block, value_block):
    key_feat = features(key_block.astype(jnp.float32)).astype(jnp.bfloat16)
    state_term = jnp.dot(key_feat.T, value_block, preferred_element_type=jnp.float32)
    norm_term = lax.optimization_barrier(jnp.sum(key_feat.astype(jnp.float32), axis=0))
    return (state_term, norm_term)

def mix_block(query_block, key_block, value_block, rim_keys, rim_values, has_prior, prior_state, prior_norm):
    length = query_block.shape[0]
    rim_width = rim_keys.shape[0]
    tile_rows = min(length, 512)
    ext_keys = jnp.concatenate([rim_keys, key_block], axis=0)
    ext_values = jnp.concatenate([rim_values, value_block], axis=0)
    query_feat = features(query_block.astype(jnp.float32))
    outputs = []
    for tile_index in range(length // tile_rows):
        row_start = tile_index * tile_rows
        query_part = query_block[row_start:row_start + tile_rows]
        win_keys = ext_keys[row_start:row_start + rim_width + tile_rows]
        win_values = ext_values[row_start:row_start + rim_width + tile_rows]
        win_scores = jnp.dot(query_part, win_keys.T, preferred_element_type=jnp.float32) * DK ** (-0.5)
        row_ids = jnp.arange(tile_rows)[:, None]
        col_ids = jnp.arange(rim_width + tile_rows)[None, :]
        visible = (col_ids > row_ids) & (col_ids <= row_ids + rim_width) & ((col_ids + row_start >= rim_width) | has_prior)
        masked = jnp.where(visible, win_scores, -jnp.inf)
        row_peak = lax.optimization_barrier(jnp.max(masked, axis=1, keepdims=True))
        raised = jnp.where(visible, jnp.exp(masked - row_peak), 0.0)
        soft_weights = (raised / lax.optimization_barrier(jnp.sum(raised, axis=1, keepdims=True))).astype(jnp.bfloat16)
        windowed = jnp.dot(soft_weights, win_values, preferred_element_type=jnp.float32)
        lin_keys = key_block[:row_start + tile_rows]
        lin_values = value_block[:row_start + tile_rows]
        lin_scores = jnp.dot(query_part, lin_keys.T, preferred_element_type=jnp.float32) * DK ** (-0.5)
        causal = jnp.arange(row_start + tile_rows)[None, :] <= row_ids + row_start
        kernel = jnp.where(causal, 1.0 + lin_scores + 0.5 * lin_scores * lin_scores, 0.0).astype(jnp.bfloat16)
        feat_part = query_feat[row_start:row_start + tile_rows]
        numerator = jnp.dot(kernel, lin_values, preferred_element_type=jnp.float32) + jnp.dot(feat_part, prior_state, precision=lax.Precision.HIGHEST)
        denominator = lax.optimization_barrier(jnp.sum(kernel.astype(jnp.float32), axis=1)) + jnp.dot(feat_part, prior_norm, precision=lax.Precision.HIGHEST)
        outputs.append(windowed + numerator / denominator[:, None])
    return jnp.concatenate(outputs, axis=0).astype(jnp.bfloat16)

def one_stream(streams):
    query_seq, key_seq, value_seq = streams
    query_blocks = query_seq.reshape(LENGTH // T_DEV, T_DEV, DK)
    key_blocks = key_seq.reshape(LENGTH // T_DEV, T_DEV, DK)
    value_blocks = value_seq.reshape(LENGTH // T_DEV, T_DEV, DV)

    def advance(running, blocks):
        prior_state, prior_norm, rim_keys, rim_values, position = running
        query_block, key_block, value_block = blocks
        result = mix_block(query_block, key_block, value_block, rim_keys, rim_values, position > 0, prior_state, prior_norm)
        state_term, norm_term = block_state(key_block, value_block)
        updated = (prior_state + state_term, prior_norm + norm_term, key_block[T_DEV - WINDOW:], value_block[T_DEV - WINDOW:], position + 1)
        return (updated, result)
    initial = (jnp.zeros((FEAT, DV), jnp.float32), jnp.zeros((FEAT,), jnp.float32), jnp.zeros((WINDOW, DK), jnp.bfloat16), jnp.zeros((WINDOW, DV), jnp.bfloat16), jnp.int32(0))
    final_carry, results = lax.scan(advance, initial, (query_blocks, key_blocks, value_blocks))
    return results.reshape(LENGTH, DV)

def reference(queries, key_vectors, value_vectors):
    query_streams = queries.reshape(BATCH, LENGTH, HEADS, DK).transpose(0, 2, 1, 3).reshape(BATCH * HEADS, LENGTH, DK)
    key_streams = key_vectors.reshape(BATCH, LENGTH, HEADS, DK).transpose(0, 2, 1, 3).reshape(BATCH * HEADS, LENGTH, DK)
    value_streams = value_vectors.reshape(BATCH, LENGTH, HEADS, DV).transpose(0, 2, 1, 3).reshape(BATCH * HEADS, LENGTH, DV)
    mixed_streams = lax.map(one_stream, (query_streams, key_streams, value_streams))
    return mixed_streams.reshape(BATCH, HEADS, LENGTH, DV).transpose(0, 2, 1, 3).reshape(BATCH, LENGTH, HEADS * DV)
```

```python
import jax
import jax.numpy as jnp
from jax import lax
from jax.experimental import pallas as pl
from jax.experimental.pallas import tpu as pltpu
from jax.sharding import PartitionSpec as P

DK = 16
DV = 128
WINDOW = 64
ROWS = 160
KEY_SUM_ROW = 137
LANES = 128
BLOCK = 256
SLOT = 32
BF16 = jnp.bfloat16
F32 = jnp.float32
MESH = pl.DeviceIdType.MESH


def iota(shape, dim):
    return lax.broadcasted_iota(jnp.int32, shape, dim)


def dot(a, b):
    return jnp.dot(a, b, preferred_element_type=F32)


def dot_nt(a, b):
    return lax.dot_general(a, b, (((1,), (1,)), ((), ())), preferred_element_type=F32)


def rolled_picker(distance, width):
    shape = (width, width)
    row, col = iota(shape, 0), iota(shape, 1)
    part = row % DK
    target = row - part + (part + distance) % DK
    hit = row * 0 + target == col
    if distance == DK // 2:
        hit = hit & (part < DK // 2)
    return jnp.where(hit, 1.0 if distance == 0 else 0.25, 0.0).astype(BF16)


def pair_picker(heads):
    above = DK * (heads - 1)
    shape = (above + DK * heads, 2 * LANES)
    row, col = iota(shape, 0) - above, iota(shape, 1)
    part, turn = col % DK, (col % LANES) // DK
    right = col >= LANES
    hit = row == jnp.where(right, (part + turn) % DK, part)
    weight = jnp.where(right, jnp.where(turn == 0, 0.0625, 0.5), 1.0)
    return jnp.where(hit, weight, 0.0).astype(BF16)


def tail_picker(group, heads):
    shape = (DK * heads, 2 * LANES)
    row, col = iota(shape, 0), iota(shape, 1)
    slot, at = (col % LANES) // SLOT, col % SLOT
    base = DK * (4 * group + slot)
    right = col >= LANES
    half = DK // 2
    left_hit = ((at < half) & (row == base + at)) | ((at >= DK) & (row == base + at - DK))
    right_hit = (at < half) & (row == base + at + half)
    picked = jnp.where(right, jnp.where(right_hit, 0.5, 0.0), jnp.where(left_hit, 1.0, 0.0))
    return picked.astype(BF16)


def kernel(
    n, heads,
    q_hbm, k_hbm, v_hbm, out_ref,
    q, kx, vx, phi_k, own, sent, prior, picker, tails, phi_q, sums, win,
    load_sem, rim_send, rim_recv, send_sem, recv_sem,
):
    rows = q.shape[0]
    width = q.shape[1]
    groups = tails.shape[0]
    place = lax.axis_index("seq")
    has_prior = place > 0
    has_next = place < n - 1
    half = LANES // 2

    loads = [
        pltpu.make_async_copy(k_hbm.at[0], kx.at[pl.ds(LANES, rows)], load_sem.at[0]),
        pltpu.make_async_copy(v_hbm.at[0], vx.at[pl.ds(LANES, rows)], load_sem.at[1]),
        pltpu.make_async_copy(q_hbm.at[0], q, load_sem.at[2]),
    ]
    for load in loads:
        load.start()

    barrier = pltpu.get_barrier_semaphore()

    @pl.when(has_prior)
    def _():
        pl.semaphore_signal(barrier, inc=1, device_id={"seq": place - 1}, device_id_type=MESH)

    rim = [
        pltpu.make_async_remote_copy(
            src_ref=src.at[0, pl.ds(rows - WINDOW, WINDOW)],
            dst_ref=dst.at[pl.ds(half, WINDOW)],
            send_sem=rim_send.at[i],
            recv_sem=rim_recv.at[i],
            device_id={"seq": place + 1},
            device_id_type=MESH,
        )
        for i, (src, dst) in enumerate(((k_hbm, kx), (v_hbm, vx)))
    ]

    def chunk(h):
        return pltpu.make_async_remote_copy(
            src_ref=sent.at[h],
            dst_ref=prior.at[h],
            send_sem=send_sem.at[h],
            recv_sem=recv_sem.at[h],
            device_id={"seq": place + 1},
            device_id_type=MESH,
        )

    @pl.when(has_next)
    def _():
        pl.semaphore_wait(barrier, 1)
        for copy in rim:
            copy.start()

    kx[0:half] = jnp.zeros((half, width), BF16)
    vx[0:half] = jnp.zeros((half, vx.shape[1]), BF16)

    @pl.when(jnp.logical_not(has_prior))
    def _():
        kx[half:LANES] = jnp.zeros((half, width), BF16)
        vx[half:LANES] = jnp.zeros((half, vx.shape[1]), BF16)
        prior[...] = jnp.zeros(prior.shape, BF16)

    picker[...] = pair_picker(heads)
    loads[0].wait()

    keys = kx[LANES:LANES + rows]
    plain = dot_nt(rolled_picker(0, width), keys)

    def put(group, block):
        block = block.astype(BF16)
        for h in range(heads):
            phi_k[h, group * DK:(group + 1) * DK, :] = block[h * DK:(h + 1) * DK]

    put(0, plain * plain)
    for distance in range(1, DK // 2 + 1):
        other = dot_nt(rolled_picker(distance, width), keys)
        product = plain * other
        if distance == DK // 2:
            one = jnp.where(iota((width, 1), 0) % DK == DK // 2, 1.0, 0.0)
            product = product + one
        put(distance, product)
    put(DK // 2 + 1, plain * 0.5)

    ones = jnp.ones((BLOCK, DV), BF16)

    def with_ones(values):
        return jnp.concatenate([values, jnp.ones((values.shape[0], DV), BF16)], axis=1)

    loads[1].wait()

    def state(h, carry):
        lanes = pl.ds(pl.multiple_of(h * DV, DV), DV)
        full = dot(phi_k[h], with_ones(vx[LANES:LANES + rows, lanes]))
        eye = iota((LANES, LANES), 0) == iota((LANES, LANES), 1)
        key_sums = full[:, DV:]
        low = jnp.sum(jnp.where(eye, key_sums[:LANES], 0.0), axis=0, keepdims=True)
        high = jnp.sum(
            jnp.where(eye[:ROWS - LANES], key_sums[LANES:], 0.0), axis=0, keepdims=True
        )
        row = iota((ROWS, DV), 0)
        term = jnp.where(
            row == KEY_SUM_ROW, low, jnp.where(row == KEY_SUM_ROW + 1, high, full[:, :DV])
        )
        own[h] = term

        @pl.when(jnp.logical_not(has_prior) & has_next)
        def _():
            sent[h] = term.astype(BF16)
            chunk(h).start()

        return carry

    lax.fori_loop(0, heads, state, 0)

    loads[2].wait()
    for group in range(groups):
        both = dot(q[...], tail_picker(group, heads))
        at = iota((1, LANES), 1) % SLOT
        left = both[:, :LANES] + jnp.where(at == DK // 2, 2.0, 0.0)
        right = both[:, LANES:] + jnp.where((at == DK // 2) | (at >= DK), 1.0, 0.0)
        tails[group] = (left * right).astype(BF16)

    @pl.when(has_prior)
    def _():
        for copy in rim:
            copy.wait_recv()

    def local(h):
        lanes = pl.ds(pl.multiple_of(h * DV, DV), DV)
        scale = jnp.where(iota((1, width), 1) // DK == h, 0.25, 0.0).astype(BF16)
        row = iota((LANES, LANES), 0)
        col = iota((LANES, LANES), 1)
        near = (col <= row) & (row - col < WINDOW)
        far = (col > row + half)[:half]
        for big in range(rows // BLOCK):
            start = big * BLOCK
            until = start + BLOCK
            queries = q[start:until] * scale
            scores = dot_nt(queries, kx[LANES:LANES + until])
            raised = scores + 1.0
            weights = raised * raised + 1.0
            causal = iota((BLOCK, BLOCK), 1) <= iota((BLOCK, BLOCK), 0)
            diagonal = jnp.where(causal, weights[:, start:], 0.0)
            if big:
                weights = jnp.concatenate([weights[:, :start], diagonal], axis=1)
            else:
                weights = diagonal
            sums[h, start:until] = dot(
                weights.astype(BF16), with_ones(vx[LANES:LANES + until, lanes])
            )
            for small in range(BLOCK // LANES):
                begin = start + small * LANES
                part = scores[small * LANES:(small + 1) * LANES]
                here = part[:, begin:begin + LANES]
                if begin:
                    before = part[:half, begin - LANES:begin]
                    seen = far
                else:
                    before = dot_nt(queries[:half], kx[0:LANES])
                    seen = far & has_prior
                here = jnp.where(near, here, -jnp.inf)
                before = jnp.where(seen, before, -jnp.inf)
                top = jnp.max(jnp.maximum(here[:half], before), axis=1, keepdims=True)
                low = jnp.max(here[half:], axis=1, keepdims=True)
                shares = jnp.concatenate(
                    [
                        jnp.concatenate(
                            [jnp.exp(before - top), jnp.zeros((half, LANES), F32)], axis=0
                        ),
                        jnp.exp(here - jnp.concatenate([top, low], axis=0)),
                    ],
                    axis=1,
                ).astype(BF16)
                both = dot(shares, with_ones(vx[begin:begin + 2 * LANES, lanes]))
                win[h, begin:begin + LANES] = both[:, :DV] / both[:, DV:]
        pick = picker[pl.ds(pl.multiple_of(DK * (heads - 1 - h), DK), width)]
        both = dot(q[...], pick)
        phi_q[h] = (both[:, :LANES] * both[:, LANES:]).astype(BF16)

    def finish(h):
        @pl.when(has_prior)
        def _():
            chunk(h).wait_recv()

            @pl.when(has_next)
            def _():
                sent[h] = (prior[h].astype(F32) + own[h]).astype(BF16)
                chunk(h).start()

        lanes = pl.ds(pl.multiple_of(h * DV, DV), DV)
        before = prior[h]
        eye = iota((LANES, LANES), 0) == iota((LANES, LANES), 1)
        wide = before[DK * 8:DK * 9].astype(F32)
        at = KEY_SUM_ROW - DK * 8
        low, high = wide[at:at + 1], wide[at + 1:at + 2]
        diagonal = jnp.concatenate(
            [jnp.where(eye, low, 0.0), jnp.where(eye[:SLOT], high, 0.0)], axis=0
        ).astype(BF16)
        key_sums = dot(diagonal, jnp.ones((LANES, DV), BF16)).astype(BF16)
        state = jnp.concatenate([before, key_sums], axis=1)
        tail = jnp.concatenate([state[LANES:]] * (LANES // SLOT), axis=0)
        slot = iota((LANES, 1), 0) // SLOT
        tail = jnp.where(slot == h % 4, tail, jnp.zeros_like(tail))
        state = jnp.concatenate([state[:LANES], tail], axis=0)
        feats = jnp.concatenate([phi_q[h], tails[h // 4]], axis=1)
        total = sums[h] + dot(feats, state)
        out_ref[0, :, lanes] = (win[h] + total[:, :DV] / total[:, DV:]).astype(BF16)

    lag = jnp.minimum(2 * jnp.maximum(place - 1, 0), heads)

    def step(t, carry):
        @pl.when(t < heads)
        def _():
            local(t)

        @pl.when((t >= lag) & (t < lag + heads))
        def _():
            finish(t - lag)

        return carry

    lax.fori_loop(0, 2 * heads, step, 0)

    @pl.when(has_next)
    def _():
        for copy in rim:
            copy.wait_send()

        def drain(h, carry):
            chunk(h).wait_send()
            return carry

        lax.fori_loop(0, heads, drain, 0)


def on_device(queries, key_vectors, value_vectors):
    n = lax.axis_size("seq")
    rows, width = queries.shape[1:]
    heads = width // DK
    values = value_vectors.shape[2]
    groups = -(-heads // 4)
    any_space = pl.BlockSpec(memory_space=pl.ANY)

    def body(*refs):
        kernel(n, heads, *refs)

    return pl.pallas_call(
        body,
        out_shape=jax.ShapeDtypeStruct((1, rows, values), BF16),
        in_specs=[any_space] * 3,
        out_specs=pl.BlockSpec(memory_space=pltpu.VMEM),
        scratch_shapes=[
            pltpu.VMEM((rows, width), BF16),
            pltpu.VMEM((LANES + rows, width), BF16),
            pltpu.VMEM((LANES + rows, values), BF16),
            pltpu.VMEM((heads, ROWS, rows), BF16),
            pltpu.VMEM((heads, ROWS, DV), F32),
            pltpu.VMEM((heads, ROWS, DV), BF16),
            pltpu.VMEM((heads, ROWS, DV), BF16),
            pltpu.VMEM((DK * (2 * heads - 1), 2 * LANES), BF16),
            pltpu.VMEM((groups, rows, LANES), BF16),
            pltpu.VMEM((heads, rows, LANES), BF16),
            pltpu.VMEM((heads, rows, 2 * DV), F32),
            pltpu.VMEM((heads, rows, DV), F32),
            pltpu.SemaphoreType.DMA((3,)),
            pltpu.SemaphoreType.DMA((2,)),
            pltpu.SemaphoreType.DMA((2,)),
            pltpu.SemaphoreType.DMA((heads,)),
            pltpu.SemaphoreType.DMA((heads,)),
        ],
        compiler_params=pltpu.CompilerParams(
            collective_id=0, has_side_effects=True, vmem_limit_bytes=48 * 2**20
        ),
    )(queries, key_vectors, value_vectors)


def solution(mesh):
    spec = P(("groups", "batch"), "seq", "head")
    return jax.shard_map(
        on_device, mesh=mesh, in_specs=(spec, spec, spec), out_specs=spec, check_vma=False
    )
```

```python
import jax
import jax.numpy as jnp
from jax import lax
from jax.experimental import pallas as pl
from jax.experimental.pallas import tpu as pltpu
from jax.sharding import PartitionSpec as P

DK = 16
DV = 128
WINDOW = 64
ROWS = 160
KEY_SUM_ROW = 137
LANES = 128
BLOCK = 256
SLOT = 32
BF16 = jnp.bfloat16
F32 = jnp.float32
MESH = pl.DeviceIdType.MESH


def iota(shape, dim):
    return lax.broadcasted_iota(jnp.int32, shape, dim)


def dot(a, b):
    return jnp.dot(a, b, preferred_element_type=F32)


def inverse(x):
    guess = pl.reciprocal(x, approx=True)
    return guess * (2.0 - x * guess)


def dot_nt(a, b):
    return lax.dot_general(a, b, (((1,), (1,)), ((), ())), preferred_element_type=F32)


def rolled_picker(distance, width):
    shape = (width, width)
    row, col = iota(shape, 0), iota(shape, 1)
    part = row & (DK - 1)
    target = row - part + ((part + distance) & (DK - 1))
    hit = target == col
    if distance == DK // 2:
        hit = hit & (part < DK // 2)
    return jnp.where(hit, 1.0 if distance == 0 else 0.25, 0.0).astype(BF16)


def pair_picker(heads):
    above = DK * (heads - 1)
    shape = (above + DK * heads, 2 * LANES)
    row, col = iota(shape, 0) - above, iota(shape, 1)
    part, turn = col & (DK - 1), (col & (LANES - 1)) >> 4
    right = col >= LANES
    hit = row == jnp.where(right, (part + turn) & (DK - 1), part)
    weight = jnp.where(right, jnp.where(turn == 0, 0.0625, 0.5), 1.0)
    return jnp.where(hit, weight, 0.0).astype(BF16)


def tail_picker(group, heads):
    shape = (DK * heads, 2 * LANES)
    row, col = iota(shape, 0), iota(shape, 1)
    slot, at = (col & (LANES - 1)) >> 5, col & (SLOT - 1)
    base = DK * (4 * group + slot)
    right = col >= LANES
    half = DK // 2
    left_hit = ((at < half) & (row == base + at)) | ((at >= DK) & (row == base + at - DK))
    right_hit = (at < half) & (row == base + at + half)
    picked = jnp.where(right, jnp.where(right_hit, 0.5, 0.0), jnp.where(left_hit, 1.0, 0.0))
    return picked.astype(BF16)


def kernel(
    n, heads,
    q_hbm, k_hbm, v_hbm, out_ref,
    q, kx, vx, phi_k, own, sent, prior, picker, tails, phi_q, sums, win,
    load_sem, rim_send, rim_recv, send_sem, recv_sem,
):
    rows = q.shape[0]
    width = q.shape[1]
    groups = tails.shape[0]
    place = lax.axis_index("seq")
    has_prior = place > 0
    has_next = place < n - 1
    half = LANES // 2

    loads = [
        pltpu.make_async_copy(k_hbm.at[0], kx.at[pl.ds(LANES, rows)], load_sem.at[0]),
        pltpu.make_async_copy(v_hbm.at[0], vx.at[pl.ds(LANES, rows)], load_sem.at[1]),
        pltpu.make_async_copy(q_hbm.at[0], q, load_sem.at[2]),
    ]
    for load in loads:
        load.start()

    barrier = pltpu.get_barrier_semaphore()

    @pl.when(has_prior)
    def _():
        pl.semaphore_signal(barrier, inc=1, device_id={"seq": place - 1}, device_id_type=MESH)

    rim = [
        pltpu.make_async_remote_copy(
            src_ref=src.at[0, pl.ds(rows - WINDOW, WINDOW)],
            dst_ref=dst.at[pl.ds(half, WINDOW)],
            send_sem=rim_send.at[i],
            recv_sem=rim_recv.at[i],
            device_id={"seq": place + 1},
            device_id_type=MESH,
        )
        for i, (src, dst) in enumerate(((k_hbm, kx), (v_hbm, vx)))
    ]

    def chunk(h):
        return pltpu.make_async_remote_copy(
            src_ref=sent.at[h],
            dst_ref=prior.at[h],
            send_sem=send_sem.at[h],
            recv_sem=recv_sem.at[h],
            device_id={"seq": place + 1},
            device_id_type=MESH,
        )

    @pl.when(has_next)
    def _():
        pl.semaphore_wait(barrier, 1)
        for copy in rim:
            copy.start()

    kx[0:half] = jnp.zeros((half, width), BF16)
    vx[0:half] = jnp.zeros((half, vx.shape[1]), BF16)

    @pl.when(jnp.logical_not(has_prior))
    def _():
        kx[half:LANES] = jnp.zeros((half, width), BF16)
        vx[half:LANES] = jnp.zeros((half, vx.shape[1]), BF16)
        prior[...] = jnp.zeros(prior.shape, BF16)

    loads[0].wait()

    keys = kx[LANES:LANES + rows]
    plain = dot_nt(rolled_picker(0, width), keys)

    def put(group, block):
        block = block.astype(BF16)
        for h in range(heads):
            phi_k[h, group * DK:(group + 1) * DK, :] = block[h * DK:(h + 1) * DK]

    put(0, plain * plain)
    for distance in range(1, DK // 2 + 1):
        other = dot_nt(rolled_picker(distance, width), keys)
        product = plain * other
        if distance == DK // 2:
            one = jnp.where(iota((width, 1), 0) & (DK - 1) == DK // 2, 1.0, 0.0)
            product = product + one
        put(distance, product)
    put(DK // 2 + 1, plain * 0.5)

    def with_ones(values):
        return jnp.concatenate([values, jnp.ones((values.shape[0], DV), BF16)], axis=1)

    loads[1].wait()

    def state(h):
        full = dot(phi_k[h], with_ones(vx[LANES:LANES + rows, h * DV:(h + 1) * DV]))
        eye = iota((LANES, LANES), 0) == (iota((LANES, LANES), 1))
        key_sums = full[:, DV:]
        low = jnp.sum(jnp.where(eye, key_sums[:LANES], 0.0), axis=0, keepdims=True)
        hit = iota((SLOT, LANES), 0) == (iota((SLOT, LANES), 1) & (SLOT - 1))
        high = jnp.sum(jnp.where(hit, key_sums[LANES:], 0.0), axis=0, keepdims=True)
        row = iota((ROWS, DV), 0)
        own[h] = jnp.where(
            row == KEY_SUM_ROW, low, jnp.where(row == KEY_SUM_ROW + 1, high, full[:, :DV])
        )

    pair = 2 - heads % 2
    for first in range(0, heads, pair):
        for h in range(first, first + pair):
            state(h)

        @pl.when(jnp.logical_not(has_prior) & has_next)
        def _():
            for h in range(first, first + pair):
                sent[h] = own[h].astype(BF16)
                chunk(h).start()

    picker[...] = pair_picker(heads)
    loads[2].wait()
    for group in range(groups):
        both = dot(q[...], tail_picker(group, heads))
        at = iota((1, LANES), 1) & (SLOT - 1)
        left = both[:, :LANES] + jnp.where(at == DK // 2, 2.0, 0.0)
        right = both[:, LANES:] + jnp.where((at == DK // 2) | (at >= DK), 1.0, 0.0)
        tails[group] = (left * right).astype(BF16)

    @pl.when(has_prior)
    def _():
        for copy in rim:
            copy.wait_recv()

    def local(h, big):
        lanes = pl.ds(pl.multiple_of(h * DV, DV), DV)
        scale = jnp.where(iota((1, width), 1) >> 4 == h, 0.25, 0.0).astype(BF16)
        row = iota((LANES, LANES), 0)
        col = iota((LANES, LANES), 1)
        near = (col <= row) & (row - col < WINDOW)
        far = (col > row + half)[:half]
        start = big * BLOCK
        until = start + BLOCK
        queries = q[start:until] * scale
        scores = dot_nt(queries, kx[LANES:LANES + until])
        raised = scores + 1.0
        weights = raised * raised + 1.0
        causal = iota((BLOCK, BLOCK), 1) <= iota((BLOCK, BLOCK), 0)
        diagonal = jnp.where(causal, weights[:, start:], 0.0)
        if big:
            weights = jnp.concatenate([weights[:, :start], diagonal], axis=1)
        else:
            weights = diagonal
        sums[h, start:until] = dot(
            weights.astype(BF16), with_ones(vx[LANES:LANES + until, lanes])
        )
        for small in range(BLOCK // LANES):
            begin = start + small * LANES
            part = scores[small * LANES:(small + 1) * LANES]
            here = part[:, begin:begin + LANES]
            if begin:
                before = part[:half, begin - LANES:begin]
                seen = far
            else:
                before = dot_nt(queries[:half], kx[0:LANES])
                seen = far & has_prior
            here = jnp.where(near, here, -jnp.inf)
            before = jnp.where(seen, before, -jnp.inf)
            top = jnp.max(jnp.maximum(here[:half], before), axis=1, keepdims=True)
            low = jnp.max(here[half:], axis=1, keepdims=True)
            shares = jnp.concatenate(
                [
                    jnp.concatenate(
                        [jnp.exp(before - top), jnp.zeros((half, LANES), F32)], axis=0
                    ),
                    jnp.exp(here - jnp.concatenate([top, low], axis=0)),
                ],
                axis=1,
            ).astype(BF16)
            both = dot(shares, with_ones(vx[begin:begin + 2 * LANES, lanes]))
            win[h, begin:begin + LANES] = both[:, :DV] * inverse(both[:, DV:])
        pick = picker[pl.ds(pl.multiple_of(DK * (heads - 1 - h), DK), width)]
        both = dot(q[start:until], pick)
        phi_q[h, start:until] = (both[:, :LANES] * both[:, LANES:]).astype(BF16)

    def forward(h):
        chunk(h).wait_recv()

        @pl.when(has_next)
        def _():
            sent[h] = (prior[h].astype(F32) + own[h]).astype(BF16)
            chunk(h).start()

    def finish(h):
        lanes = pl.ds(pl.multiple_of(h * DV, DV), DV)
        before = prior[h]
        wide = before[DK * 8:DK * 9].astype(F32)
        at = KEY_SUM_ROW - DK * 8
        lane = iota((1, LANES), 1)
        high = jnp.where(lane >> 5 == (h & 3), wide[at + 1:at + 2], 0.0)
        key_sums = jnp.concatenate([wide[at:at + 1], high], axis=1).astype(BF16)
        key_sums = jnp.broadcast_to(key_sums, (DV, 2 * LANES))
        tail = jnp.concatenate([before[LANES:]] * (LANES // SLOT), axis=0)
        slot = iota((LANES, 1), 0) >> 5
        tail = jnp.where(slot == (h & 3), tail, jnp.zeros_like(tail))
        state = jnp.concatenate([before[:LANES], tail], axis=0)
        feats = jnp.concatenate([phi_q[h], tails[h >> 2]], axis=1)
        total = sums[h, :, :DV] + dot(feats, state)
        weight = sums[h, :, DV:] + dot_nt(feats, key_sums)
        out_ref[0, :, lanes] = (win[h] + total * inverse(weight)).astype(BF16)

    blocks = rows // BLOCK
    late = jnp.minimum(jnp.maximum(place - 1, 0), heads // 2)
    receive_lag = 4 * late + 1
    finish_lag = 2 * late

    def step(t, carry):
        for big in range(blocks):
            @pl.when(t < heads)
            def _():
                local(t, big)

            arriving = blocks * t + big - receive_lag

            @pl.when(has_prior & (arriving >= 0) & (arriving < heads))
            def _():
                forward(arriving)

        @pl.when((t >= finish_lag) & (t < finish_lag + heads))
        def _():
            finish(t - finish_lag)

        return carry

    lax.fori_loop(0, 2 * heads, step, 0)

    @pl.when(has_next)
    def _():
        for copy in rim:
            copy.wait_send()

        def drain(h, carry):
            chunk(h).wait_send()
            return carry

        lax.fori_loop(0, heads, drain, 0)


def on_device(queries, key_vectors, value_vectors):
    n = lax.axis_size("seq")
    rows, width = queries.shape[1:]
    heads = width // DK
    values = value_vectors.shape[2]
    groups = -(-heads // 4)
    any_space = pl.BlockSpec(memory_space=pl.ANY)

    def body(*refs):
        kernel(n, heads, *refs)

    return pl.pallas_call(
        body,
        out_shape=jax.ShapeDtypeStruct((1, rows, values), BF16),
        in_specs=[any_space] * 3,
        out_specs=pl.BlockSpec(memory_space=pltpu.VMEM),
        scratch_shapes=[
            pltpu.VMEM((rows, width), BF16),
            pltpu.VMEM((LANES + rows, width), BF16),
            pltpu.VMEM((LANES + rows, values), BF16),
            pltpu.VMEM((heads, ROWS, rows), BF16),
            pltpu.VMEM((heads, ROWS, DV), F32),
            pltpu.VMEM((heads, ROWS, DV), BF16),
            pltpu.VMEM((heads, ROWS, DV), BF16),
            pltpu.VMEM((DK * (2 * heads - 1), 2 * LANES), BF16),
            pltpu.VMEM((groups, rows, LANES), BF16),
            pltpu.VMEM((heads, rows, LANES), BF16),
            pltpu.VMEM((heads, rows, 2 * DV), F32),
            pltpu.VMEM((heads, rows, DV), F32),
            pltpu.SemaphoreType.DMA((3,)),
            pltpu.SemaphoreType.DMA((2,)),
            pltpu.SemaphoreType.DMA((2,)),
            pltpu.SemaphoreType.DMA((heads,)),
            pltpu.SemaphoreType.DMA((heads,)),
        ],
        compiler_params=pltpu.CompilerParams(
            collective_id=0, has_side_effects=True, vmem_limit_bytes=48 * 2**20
        ),
    )(*[pltpu.with_memory_space_constraint(x, pltpu.HBM) for x in (queries, key_vectors, value_vectors)])


def solution(mesh):
    spec = P(("groups", "batch"), "seq", "head")
    return jax.shard_map(
        on_device, mesh=mesh, in_specs=(spec, spec, spec), out_specs=spec, check_vma=False
    )
```

```python
import jax
import jax.numpy as jnp
from jax import lax
from jax.experimental import pallas as pl
from jax.experimental.pallas import tpu as pltpu
from jax.sharding import PartitionSpec as P

DK = 16
DV = 128
WINDOW = 64
ROWS = 160
KEY_SUM_ROW = 137
LANES = 128
BLOCK = 256
SLOT = 32
BF16 = jnp.bfloat16
F32 = jnp.float32
MESH = pl.DeviceIdType.MESH


def iota(shape, dim):
    return lax.broadcasted_iota(jnp.int32, shape, dim)


def dot(a, b):
    return jnp.dot(a, b, preferred_element_type=F32)


def inverse(x):
    guess = pl.reciprocal(x, approx=True)
    return guess * (2.0 - x * guess)


def dot_nt(a, b):
    return lax.dot_general(a, b, (((1,), (1,)), ((), ())), preferred_element_type=F32)


def rolled_picker(distance, width):
    shape = (width, width)
    row, col = iota(shape, 0), iota(shape, 1)
    part = row & (DK - 1)
    target = row - part + ((part + distance) & (DK - 1))
    hit = target == col
    if distance == DK // 2:
        hit = hit & (part < DK // 2)
    return jnp.where(hit, 1.0 if distance == 0 else 0.25, 0.0).astype(BF16)


def pair_picker(heads):
    above = DK * (heads - 1)
    shape = (above + DK * heads, 2 * LANES)
    row, col = iota(shape, 0) - above, iota(shape, 1)
    part, turn = col & (DK - 1), (col & (LANES - 1)) >> 4
    right = col >= LANES
    hit = row == jnp.where(right, (part + turn) & (DK - 1), part)
    weight = jnp.where(right, jnp.where(turn == 0, 0.0625, 0.5), 1.0)
    return jnp.where(hit, weight, 0.0).astype(BF16)


def tail_picker(group, heads):
    shape = (DK * heads, 2 * LANES)
    row, col = iota(shape, 0), iota(shape, 1)
    slot, at = (col & (LANES - 1)) >> 5, col & (SLOT - 1)
    base = DK * (4 * group + slot)
    right = col >= LANES
    half = DK // 2
    left_hit = ((at < half) & (row == base + at)) | ((at >= DK) & (row == base + at - DK))
    right_hit = (at < half) & (row == base + at + half)
    picked = jnp.where(right, jnp.where(right_hit, 0.5, 0.0), jnp.where(left_hit, 1.0, 0.0))
    return picked.astype(BF16)


def kernel(
    n, heads,
    q_hbm, k_hbm, v_hbm, out_ref,
    q, kx, vx, phi_k, own, sent, prior, picker, tails, phi_q, sums, win,
    load_sem, rim_send, rim_recv, send_sem, recv_sem,
):
    rows = q.shape[0]
    width = q.shape[1]
    groups = tails.shape[0]
    place = lax.axis_index("seq")
    has_prior = place > 0
    has_next = place < n - 1
    half = LANES // 2

    loads = [
        pltpu.make_async_copy(k_hbm.at[0], kx.at[pl.ds(LANES, rows)], load_sem.at[0]),
        pltpu.make_async_copy(v_hbm.at[0], vx.at[pl.ds(LANES, rows)], load_sem.at[1]),
        pltpu.make_async_copy(q_hbm.at[0], q, load_sem.at[2]),
    ]
    for load in loads:
        load.start()

    barrier = pltpu.get_barrier_semaphore()

    @pl.when(has_prior)
    def _():
        pl.semaphore_signal(barrier, inc=1, device_id={"seq": place - 1}, device_id_type=MESH)

    rim = [
        pltpu.make_async_remote_copy(
            src_ref=src.at[0, pl.ds(rows - WINDOW, WINDOW)],
            dst_ref=dst.at[pl.ds(half, WINDOW)],
            send_sem=rim_send.at[i],
            recv_sem=rim_recv.at[i],
            device_id={"seq": place + 1},
            device_id_type=MESH,
        )
        for i, (src, dst) in enumerate(((k_hbm, kx), (v_hbm, vx)))
    ]

    def chunk(h):
        return pltpu.make_async_remote_copy(
            src_ref=sent.at[h],
            dst_ref=prior.at[h],
            send_sem=send_sem.at[h],
            recv_sem=recv_sem.at[h],
            device_id={"seq": place + 1},
            device_id_type=MESH,
        )

    @pl.when(has_next)
    def _():
        pl.semaphore_wait(barrier, 1)

    @pl.when(has_prior & has_next)
    def _():
        for copy in rim:
            copy.start()

    kx[0:half] = jnp.zeros((half, width), BF16)
    vx[0:half] = jnp.zeros((half, vx.shape[1]), BF16)

    @pl.when(jnp.logical_not(has_prior))
    def _():
        kx[half:LANES] = jnp.zeros((half, width), BF16)
        vx[half:LANES] = jnp.zeros((half, vx.shape[1]), BF16)
        prior[...] = jnp.zeros(prior.shape, BF16)

    loads[0].wait()

    keys = kx[LANES:LANES + rows]
    plain = dot_nt(rolled_picker(0, width), keys)

    def put(group, block):
        block = block.astype(BF16)
        for h in range(heads):
            phi_k[h, group * DK:(group + 1) * DK, :] = block[h * DK:(h + 1) * DK]

    put(0, plain * plain)
    for distance in range(1, DK // 2 + 1):
        other = dot_nt(rolled_picker(distance, width), keys)
        product = plain * other
        if distance == DK // 2:
            one = jnp.where(iota((width, 1), 0) & (DK - 1) == DK // 2, 1.0, 0.0)
            product = product + one
        put(distance, product)
    put(DK // 2 + 1, plain * 0.5)

    def with_ones(values):
        return jnp.concatenate([values, jnp.ones((values.shape[0], DV), BF16)], axis=1)

    loads[1].wait()

    def state(h):
        full = dot(phi_k[h], with_ones(vx[LANES:LANES + rows, h * DV:(h + 1) * DV]))
        eye = iota((LANES, LANES), 0) == (iota((LANES, LANES), 1))
        key_sums = full[:, DV:]
        low = jnp.sum(jnp.where(eye, key_sums[:LANES], 0.0), axis=0, keepdims=True)
        hit = iota((SLOT, LANES), 0) == (iota((SLOT, LANES), 1) & (SLOT - 1))
        high = jnp.sum(jnp.where(hit, key_sums[LANES:], 0.0), axis=0, keepdims=True)
        row = iota((ROWS, DV), 0)
        own[h] = jnp.where(
            row == KEY_SUM_ROW, low, jnp.where(row == KEY_SUM_ROW + 1, high, full[:, :DV])
        )

    pair = 2 - heads % 2
    for first in range(0, heads, pair):
        for h in range(first, first + pair):
            state(h)

        @pl.when(jnp.logical_not(has_prior) & has_next)
        def _():
            for h in range(first, first + pair):
                sent[h] = own[h].astype(BF16)
                chunk(h).start()

    @pl.when(jnp.logical_not(has_prior) & has_next)
    def _():
        for copy in rim:
            copy.start()

    picker[...] = pair_picker(heads)
    loads[2].wait()
    for group in range(groups):
        both = dot(q[...], tail_picker(group, heads))
        at = iota((1, LANES), 1) & (SLOT - 1)
        left = both[:, :LANES] + jnp.where(at == DK // 2, 2.0, 0.0)
        right = both[:, LANES:] + jnp.where((at == DK // 2) | (at >= DK), 1.0, 0.0)
        tails[group] = (left * right).astype(BF16)

    row = iota((LANES, LANES), 0)
    col = iota((LANES, LANES), 1)

    def head_scale(h):
        return jnp.where(iota((1, width), 1) >> 4 == h, 0.25, 0.0).astype(BF16)

    def lanes_of(h):
        return pl.ds(pl.multiple_of(h * DV, DV), DV)

    def local(members, big):
        near = (col <= row) & (row - col < WINDOW)
        far = (col > row + half)[:half]
        start = big * BLOCK
        until = start + BLOCK
        causal = iota((BLOCK, BLOCK), 1) <= iota((BLOCK, BLOCK), 0)
        scores = [
            dot_nt(q[start:until] * head_scale(h), kx[LANES:LANES + until]) for h in members
        ]
        chains = []
        for h, score in zip(members, scores):
            for small in range(BLOCK // LANES):
                begin = start + small * LANES
                part = score[small * LANES:(small + 1) * LANES]
                here = jnp.where(near, part[:, begin:begin + LANES], -jnp.inf)
                low = jnp.max(here[half:], axis=1, keepdims=True)
                if begin:
                    before = jnp.where(far, part[:half, begin - LANES:begin], -jnp.inf)
                    top = jnp.max(jnp.maximum(here[:half], before), axis=1, keepdims=True)
                    chains.append((h, begin, here, before, top, low))
                else:
                    chains.append((h, begin, here, None, None, low))
        for h, score in zip(members, scores):
            raised = score + 1.0
            weights = raised * raised + 1.0
            diagonal = jnp.where(causal, weights[:, start:], 0.0)
            if big:
                weights = jnp.concatenate([weights[:, :start], diagonal], axis=1)
            else:
                weights = diagonal
            sums[h, start:until] = dot(
                weights.astype(BF16), with_ones(vx[LANES:LANES + until, lanes_of(h)])
            )
        shares = []
        for h, begin, here, before, top, low in chains:
            if begin:
                share = jnp.concatenate(
                    [
                        jnp.concatenate(
                            [jnp.exp(before - top), jnp.zeros((half, LANES), F32)], axis=0
                        ),
                        jnp.exp(here - jnp.concatenate([top, low], axis=0)),
                    ],
                    axis=1,
                )
            else:
                share = jnp.exp(here[half:] - low)
            shares.append(share.astype(BF16))
        windows = []
        for (h, begin, *_), share in zip(chains, shares):
            first = begin if begin else LANES
            windows.append(
                dot(share, with_ones(vx[first:begin + 2 * LANES, lanes_of(h)]))
            )
        for h in members:
            pick = picker[pl.ds(pl.multiple_of(DK * (heads - 1 - h), DK), width)]
            both = dot(q[start:until], pick)
            phi_q[h, start:until] = (both[:, :LANES] * both[:, LANES:]).astype(BF16)
        for (h, begin, *_), both in zip(chains, windows):
            first = begin if begin else half
            win[h, first:begin + LANES] = both[:, :DV] * inverse(both[:, DV:])

    def edge():
        queries = jnp.concatenate([q[0:half] * head_scale(h) for h in range(heads)], axis=0)
        scores = dot_nt(queries, kx[0:2 * LANES])
        at = iota((half, 2 * LANES), 1)
        line = iota((half, 2 * LANES), 0)
        seen = (at > line + half) & (at <= line + LANES) & ((at >= LANES) | has_prior)
        shares = []
        for h in range(heads):
            score = jnp.where(seen, scores[h * half:(h + 1) * half], -jnp.inf)
            peak = jnp.max(
                jnp.maximum(score[:, :LANES], score[:, LANES:]), axis=1, keepdims=True
            )
            shares.append(jnp.exp(score - peak).astype(BF16))
        for h in range(heads):
            both = dot(shares[h], with_ones(vx[0:2 * LANES, h * DV:(h + 1) * DV]))
            win[h, 0:half] = both[:, :DV] * inverse(both[:, DV:])

    def forward(h):
        @pl.when(has_prior & (h >= 0) & (h < heads))
        def _():
            chunk(h).wait_recv()

            @pl.when(has_next)
            def _():
                sent[h] = (prior[h].astype(F32) + own[h]).astype(BF16)
                chunk(h).start()

    def finish(members):
        totals = []
        for h in members:
            before = prior[h]
            wide = before[DK * 8:DK * 9].astype(F32)
            at = KEY_SUM_ROW - DK * 8
            lane = iota((1, LANES), 1)
            high = jnp.where(lane >> 5 == (h & 3), wide[at + 1:at + 2], 0.0)
            key_sums = jnp.concatenate([wide[at:at + 1], high], axis=1).astype(BF16)
            key_sums = jnp.broadcast_to(key_sums, (DV, 2 * LANES))
            tail = jnp.concatenate([before[LANES:]] * (LANES // SLOT), axis=0)
            slot = iota((LANES, 1), 0) >> 5
            tail = jnp.where(slot == (h & 3), tail, jnp.zeros_like(tail))
            state = jnp.concatenate([before[:LANES], tail], axis=0)
            feats = jnp.concatenate([phi_q[h], tails[h >> 2]], axis=1)
            totals.append((dot(feats, state), dot_nt(feats, key_sums)))
        for h, (total, weight) in zip(members, totals):
            total = sums[h, :, :DV] + total
            weight = sums[h, :, DV:] + weight
            out_ref[0, :, lanes_of(h)] = (win[h] + total * inverse(weight)).astype(BF16)

    blocks = rows // BLOCK
    steps = heads // pair
    units = blocks * steps
    late = jnp.maximum(place - 1, 0)
    lag = jnp.minimum(1 + 2 * late, units + 1)

    def spread(t, carry):
        members = [pair * t + e for e in range(pair)]
        for order in range(blocks):
            local(members, blocks - 1 - order)
            forward(blocks * t + order - lag)
        return carry

    lax.fori_loop(0, steps, spread, 0)
    forward(units - lag)

    @pl.when(has_prior)
    def _():
        for copy in rim:
            copy.wait_recv()

    edge()

    def gather(t, carry):
        members = [pair * t + e for e in range(pair)]
        for h in members:
            forward(units + 1 - lag + h)
        finish(members)
        return carry

    lax.fori_loop(0, steps, gather, 0)

    @pl.when(has_next)
    def _():
        for copy in rim:
            copy.wait_send()

        def drain(h, carry):
            chunk(h).wait_send()
            return carry

        lax.fori_loop(0, heads, drain, 0)


def on_device(queries, key_vectors, value_vectors):
    n = lax.axis_size("seq")
    rows, width = queries.shape[1:]
    heads = width // DK
    values = value_vectors.shape[2]
    groups = -(-heads // 4)
    any_space = pl.BlockSpec(memory_space=pl.ANY)

    def body(*refs):
        kernel(n, heads, *refs)

    return pl.pallas_call(
        body,
        out_shape=jax.ShapeDtypeStruct((1, rows, values), BF16),
        in_specs=[any_space] * 3,
        out_specs=pl.BlockSpec(memory_space=pltpu.VMEM),
        scratch_shapes=[
            pltpu.VMEM((rows, width), BF16),
            pltpu.VMEM((LANES + rows, width), BF16),
            pltpu.VMEM((LANES + rows, values), BF16),
            pltpu.VMEM((heads, ROWS, rows), BF16),
            pltpu.VMEM((heads, ROWS, DV), F32),
            pltpu.VMEM((heads, ROWS, DV), BF16),
            pltpu.VMEM((heads, ROWS, DV), BF16),
            pltpu.VMEM((DK * (2 * heads - 1), 2 * LANES), BF16),
            pltpu.VMEM((groups, rows, LANES), BF16),
            pltpu.VMEM((heads, rows, LANES), BF16),
            pltpu.VMEM((heads, rows, 2 * DV), F32),
            pltpu.VMEM((heads, rows, DV), F32),
            pltpu.SemaphoreType.DMA((3,)),
            pltpu.SemaphoreType.DMA((2,)),
            pltpu.SemaphoreType.DMA((2,)),
            pltpu.SemaphoreType.DMA((heads,)),
            pltpu.SemaphoreType.DMA((heads,)),
        ],
        compiler_params=pltpu.CompilerParams(
            collective_id=0, has_side_effects=True, vmem_limit_bytes=48 * 2**20
        ),
    )(*[pltpu.with_memory_space_constraint(x, pltpu.HBM) for x in (queries, key_vectors, value_vectors)])


def solution(mesh):
    spec = P(("groups", "batch"), "seq", "head")
    return jax.shard_map(
        on_device, mesh=mesh, in_specs=(spec, spec, spec), out_specs=spec, check_vma=False
    )
```

```python
import jax
import jax.numpy as jnp
from jax import lax
from jax.experimental import pallas as pl
from jax.experimental.pallas import tpu as pltpu
from jax.sharding import PartitionSpec as P

DK = 16
DV = 128
WINDOW = 64
ROWS = 160
KEY_SUM_ROW = 137
PIECES = 1
LANES = 128
BLOCK = 256
SLOT = 32
BF16 = jnp.bfloat16
F32 = jnp.float32
MESH = pl.DeviceIdType.MESH


def iota(shape, dim):
    return lax.broadcasted_iota(jnp.int32, shape, dim)


def dot(a, b):
    return jnp.dot(a, b, preferred_element_type=F32)


def inverse(x):
    guess = pl.reciprocal(x, approx=True)
    return guess * (2.0 - x * guess)


def dot_nt(a, b):
    return lax.dot_general(a, b, (((1,), (1,)), ((), ())), preferred_element_type=F32)


def rolled_picker(distance, width):
    shape = (width, width)
    row, col = iota(shape, 0), iota(shape, 1)
    part = row & (DK - 1)
    target = row - part + ((part + distance) & (DK - 1))
    hit = target == col
    if distance == DK // 2:
        hit = hit & (part < DK // 2)
    return jnp.where(hit, 1.0 if distance == 0 else 0.25, 0.0).astype(BF16)


def pair_picker(heads):
    above = DK * (heads - 1)
    shape = (above + DK * heads, 2 * LANES)
    row, col = iota(shape, 0) - above, iota(shape, 1)
    part, turn = col & (DK - 1), (col & (LANES - 1)) >> 4
    right = col >= LANES
    hit = row == jnp.where(right, (part + turn) & (DK - 1), part)
    weight = jnp.where(right, jnp.where(turn == 0, 0.0625, 0.5), 1.0)
    return jnp.where(hit, weight, 0.0).astype(BF16)


def tail_picker(group, heads):
    shape = (DK * heads, 2 * LANES)
    row, col = iota(shape, 0), iota(shape, 1)
    slot, at = (col & (LANES - 1)) >> 5, col & (SLOT - 1)
    base = DK * (4 * group + slot)
    right = col >= LANES
    half = DK // 2
    left_hit = ((at < half) & (row == base + at)) | ((at >= DK) & (row == base + at - DK))
    right_hit = (at < half) & (row == base + at + half)
    picked = jnp.where(right, jnp.where(right_hit, 0.5, 0.0), jnp.where(left_hit, 1.0, 0.0))
    return picked.astype(BF16)


def kernel(
    n, heads,
    q_hbm, k_hbm, v_hbm, out_ref,
    q, kx, vx, phi_k, own, sent, prior, picker, tails, phi_q, sums, win, rim_win,
    load_sem, rim_send, rim_recv, send_sem, recv_sem,
):
    rows = q.shape[0]
    width = q.shape[1]
    groups = tails.shape[0]
    place = lax.axis_index("seq")
    has_prior = place > 0
    has_next = place < n - 1
    half = LANES // 2

    loads = [
        pltpu.make_async_copy(k_hbm.at[0], kx.at[pl.ds(LANES, rows)], load_sem.at[0]),
        pltpu.make_async_copy(v_hbm.at[0], vx.at[pl.ds(LANES, rows)], load_sem.at[1]),
        pltpu.make_async_copy(q_hbm.at[0], q, load_sem.at[2]),
    ]
    for load in loads:
        load.start()

    barrier = pltpu.get_barrier_semaphore()

    @pl.when(has_prior)
    def _():
        pl.semaphore_signal(barrier, inc=1, device_id={"seq": place - 1}, device_id_type=MESH)

    rim = [
        pltpu.make_async_remote_copy(
            src_ref=src.at[0, pl.ds(rows - WINDOW, WINDOW)],
            dst_ref=dst.at[pl.ds(half, WINDOW)],
            send_sem=rim_send.at[i],
            recv_sem=rim_recv.at[i],
            device_id={"seq": place + 1},
            device_id_type=MESH,
        )
        for i, (src, dst) in enumerate(((k_hbm, kx), (v_hbm, vx)))
    ]

    def chunk(h, piece):
        lines = pl.ds(piece * (ROWS // PIECES), ROWS // PIECES)
        return pltpu.make_async_remote_copy(
            src_ref=sent.at[h, lines],
            dst_ref=prior.at[h, lines],
            send_sem=send_sem.at[h, piece],
            recv_sem=recv_sem.at[h, piece],
            device_id={"seq": place + 1},
            device_id_type=MESH,
        )

    kx[0:half] = jnp.zeros((half, width), BF16)
    vx[0:half] = jnp.zeros((half, vx.shape[1]), BF16)

    @pl.when(jnp.logical_not(has_prior))
    def _():
        kx[half:LANES] = jnp.zeros((half, width), BF16)
        vx[half:LANES] = jnp.zeros((half, vx.shape[1]), BF16)
        prior[...] = jnp.zeros(prior.shape, BF16)

    loads[0].wait()

    keys = kx[LANES:LANES + rows]
    plain = dot_nt(rolled_picker(0, width), keys)

    def put(group, block):
        block = block.astype(BF16)
        for h in range(heads):
            phi_k[h, group * DK:(group + 1) * DK, :] = block[h * DK:(h + 1) * DK]

    put(0, plain * plain)
    for distance in range(1, DK // 2 + 1):
        other = dot_nt(rolled_picker(distance, width), keys)
        product = plain * other
        if distance == DK // 2:
            one = jnp.where(iota((width, 1), 0) & (DK - 1) == DK // 2, 1.0, 0.0)
            product = product + one
        put(distance, product)
    put(DK // 2 + 1, plain * 0.5)

    def with_ones(values):
        return jnp.concatenate([values, jnp.ones((values.shape[0], DV), BF16)], axis=1)

    @pl.when(has_next)
    def _():
        pl.semaphore_wait(barrier, 1)

    @pl.when(has_prior & has_next)
    def _():
        for copy in rim:
            copy.start()

    loads[1].wait()

    def state(h):
        full = dot(phi_k[h], with_ones(vx[LANES:LANES + rows, h * DV:(h + 1) * DV]))
        eye = iota((LANES, LANES), 0) == (iota((LANES, LANES), 1))
        key_sums = full[:, DV:]
        low = jnp.sum(jnp.where(eye, key_sums[:LANES], 0.0), axis=0, keepdims=True)
        hit = iota((SLOT, LANES), 0) == (iota((SLOT, LANES), 1) & (SLOT - 1))
        high = jnp.sum(jnp.where(hit, key_sums[LANES:], 0.0), axis=0, keepdims=True)
        row = iota((ROWS, DV), 0)
        own[h] = jnp.where(
            row == KEY_SUM_ROW, low, jnp.where(row == KEY_SUM_ROW + 1, high, full[:, :DV])
        )

    pair = 2 - heads % 2
    for first in range(0, heads, pair):
        for h in range(first, first + pair):
            state(h)

        @pl.when(jnp.logical_not(has_prior) & has_next)
        def _():
            for h in range(first, first + pair):
                sent[h] = own[h].astype(BF16)
                for piece in range(PIECES):
                    chunk(h, piece).start()

    picker[...] = pair_picker(heads)
    loads[2].wait()
    for group in range(groups):
        both = dot(q[...], tail_picker(group, heads))
        at = iota((1, LANES), 1) & (SLOT - 1)
        left = both[:, :LANES] + jnp.where(at == DK // 2, 2.0, 0.0)
        right = both[:, LANES:] + jnp.where((at == DK // 2) | (at >= DK), 1.0, 0.0)
        tails[group] = (left * right).astype(BF16)

    row = iota((LANES, LANES), 0)
    col = iota((LANES, LANES), 1)

    def head_scale(h):
        return jnp.where(iota((1, width), 1) >> 4 == h, 0.25, 0.0).astype(BF16)

    def lanes_of(h):
        return pl.ds(pl.multiple_of(h * DV, DV), DV)

    def local(members, big):
        near = (col <= row) & (row - col < WINDOW)
        far = (col > row + half)[:half]
        start = big * BLOCK
        until = start + BLOCK
        causal = iota((BLOCK, BLOCK), 1) <= iota((BLOCK, BLOCK), 0)
        scores = [
            dot_nt(q[start:until] * head_scale(h), kx[LANES:LANES + until]) for h in members
        ]
        chains = []
        for h, score in zip(members, scores):
            for small in range(BLOCK // LANES):
                begin = start + small * LANES
                part = score[small * LANES:(small + 1) * LANES]
                here = jnp.where(near, part[:, begin:begin + LANES], -jnp.inf)
                low = jnp.max(here[half:], axis=1, keepdims=True)
                if begin:
                    before = jnp.where(far, part[:half, begin - LANES:begin], -jnp.inf)
                    top = jnp.max(jnp.maximum(here[:half], before), axis=1, keepdims=True)
                    chains.append((h, begin, here, before, top, low))
                else:
                    chains.append((h, begin, here, None, None, low))
        for h, score in zip(members, scores):
            raised = score + 1.0
            weights = raised * raised + 1.0
            diagonal = jnp.where(causal, weights[:, start:], 0.0)
            if big:
                weights = jnp.concatenate([weights[:, :start], diagonal], axis=1)
            else:
                weights = diagonal
            sums[h, start:until] = dot(
                weights.astype(BF16), with_ones(vx[LANES:LANES + until, lanes_of(h)])
            )
        shares = []
        for h, begin, here, before, top, low in chains:
            if begin:
                share = jnp.concatenate(
                    [
                        jnp.concatenate(
                            [jnp.exp(before - top), jnp.zeros((half, LANES), F32)], axis=0
                        ),
                        jnp.exp(here - jnp.concatenate([top, low], axis=0)),
                    ],
                    axis=1,
                )
            else:
                share = jnp.exp(here[half:] - low)
            shares.append(share.astype(BF16))
        windows = []
        for (h, begin, *_), share in zip(chains, shares):
            first = begin if begin else LANES
            windows.append(
                dot(share, with_ones(vx[first:begin + 2 * LANES, lanes_of(h)]))
            )
        for h in members:
            pick = picker[pl.ds(pl.multiple_of(DK * (heads - 1 - h), DK), width)]
            both = dot(q[start:until], pick)
            phi_q[h, start:until] = (both[:, :LANES] * both[:, LANES:]).astype(BF16)
        for (h, begin, *_), both in zip(chains, windows):
            first = begin if begin else half
            win[h, first:begin + LANES] = both[:, :DV] * inverse(both[:, DV:])

    def edge():
        queries = jnp.concatenate([q[0:half] * head_scale(h) for h in range(heads)], axis=0)
        scores = dot_nt(queries, kx[0:2 * LANES])
        at = iota((half, 2 * LANES), 1)
        line = iota((half, 2 * LANES), 0)
        seen = (at > line + half) & (at <= line + LANES) & ((at >= LANES) | has_prior)
        shares = []
        for h in range(heads):
            score = jnp.where(seen, scores[h * half:(h + 1) * half], -jnp.inf)
            peak = jnp.max(
                jnp.maximum(score[:, :LANES], score[:, LANES:]), axis=1, keepdims=True
            )
            shares.append(jnp.exp(score - peak).astype(BF16))
        for h in range(heads):
            both = dot(shares[h], with_ones(vx[0:2 * LANES, h * DV:(h + 1) * DV]))
            rim_win[h] = both[:, :DV] * inverse(both[:, DV:])

    def forward(first, end):
        def one(h, carry):
            for piece in range(PIECES):
                chunk(h, piece).wait_recv()
                lines = slice(piece * (ROWS // PIECES), (piece + 1) * (ROWS // PIECES))

                @pl.when(has_next)
                def _():
                    sent[h, lines] = (prior[h, lines].astype(F32) + own[h, lines]).astype(BF16)
                    chunk(h, piece).start()

            return carry

        @pl.when(has_prior)
        def _():
            lax.fori_loop(first, end, one, 0)

    def finish(members):
        totals = []
        for h in members:
            before = prior[h]
            wide = before[DK * 8:DK * 9].astype(F32)
            at = KEY_SUM_ROW - DK * 8
            lane = iota((1, LANES), 1)
            high = jnp.where(lane >> 5 == (h & 3), wide[at + 1:at + 2], 0.0)
            key_sums = jnp.concatenate([wide[at:at + 1], high], axis=1).astype(BF16)
            key_sums = jnp.broadcast_to(key_sums, (DV, 2 * LANES))
            tail = jnp.concatenate([before[LANES:]] * (LANES // SLOT), axis=0)
            slot = iota((LANES, 1), 0) >> 5
            tail = jnp.where(slot == (h & 3), tail, jnp.zeros_like(tail))
            state = jnp.concatenate([before[:LANES], tail], axis=0)
            feats = jnp.concatenate([phi_q[h], tails[h >> 2]], axis=1)
            totals.append((dot(feats, state), dot_nt(feats, key_sums)))
        for h, (total, weight) in zip(members, totals):
            total = sums[h, :, :DV] + total
            weight = sums[h, :, DV:] + weight
            linear = total * inverse(weight)
            win[h, 0:half] = linear[0:half]
            out_ref[0, half:rows, lanes_of(h)] = (win[h, half:rows] + linear[half:]).astype(BF16)

    blocks = rows // BLOCK
    steps = heads // pair
    units = blocks * steps
    delay = jnp.where(has_next, 10 + 10 * jnp.maximum(place - 1, 0), 1000)

    def due(unit):
        return jnp.minimum(jnp.maximum(5 * (unit + 1) - delay, 0) // 4, heads)

    def needed(t):
        return jnp.maximum(pair * t, due(units + t))

    def spread(t, carry):
        members = [pair * t + e for e in range(pair)]
        for order in range(blocks):
            local(members, blocks - 1 - order)
            unit = blocks * t + order
            forward(due(unit - 1), due(unit))
        return carry

    lax.fori_loop(0, steps, spread, 0)
    forward(due(units - 1), due(units))

    @pl.when(jnp.logical_not(has_prior) & has_next)
    def _():
        for copy in rim:
            copy.start()

    rim_late = place == 1

    @pl.when(has_prior & jnp.logical_not(rim_late))
    def _():
        for copy in rim:
            copy.wait_recv()

    @pl.when(jnp.logical_not(rim_late))
    def _():
        edge()

    def gather(t, carry):
        members = [pair * t + e for e in range(pair)]
        forward(needed(t), needed(t + 1))
        finish(members)
        return carry

    lax.fori_loop(0, steps, gather, 0)

    @pl.when(rim_late)
    def _():
        for copy in rim:
            copy.wait_recv()
        edge()

    for h in range(heads):
        out_ref[0, 0:half, h * DV:(h + 1) * DV] = (rim_win[h] + win[h, 0:half]).astype(BF16)

    @pl.when(has_next)
    def _():
        for copy in rim:
            copy.wait_send()

        def drain(h, carry):
            for piece in range(PIECES):
                chunk(h, piece).wait_send()
            return carry

        lax.fori_loop(0, heads, drain, 0)


def on_device(queries, key_vectors, value_vectors):
    n = lax.axis_size("seq")
    rows, width = queries.shape[1:]
    heads = width // DK
    values = value_vectors.shape[2]
    groups = -(-heads // 4)
    any_space = pl.BlockSpec(memory_space=pl.ANY)

    def body(*refs):
        kernel(n, heads, *refs)

    return pl.pallas_call(
        body,
        out_shape=jax.ShapeDtypeStruct((1, rows, values), BF16),
        in_specs=[any_space] * 3,
        out_specs=pl.BlockSpec(memory_space=pltpu.VMEM),
        scratch_shapes=[
            pltpu.VMEM((rows, width), BF16),
            pltpu.VMEM((LANES + rows, width), BF16),
            pltpu.VMEM((LANES + rows, values), BF16),
            pltpu.VMEM((heads, ROWS, rows), BF16),
            pltpu.VMEM((heads, ROWS, DV), F32),
            pltpu.VMEM((heads, ROWS, DV), BF16),
            pltpu.VMEM((heads, ROWS, DV), BF16),
            pltpu.VMEM((DK * (2 * heads - 1), 2 * LANES), BF16),
            pltpu.VMEM((groups, rows, LANES), BF16),
            pltpu.VMEM((heads, rows, LANES), BF16),
            pltpu.VMEM((heads, rows, 2 * DV), F32),
            pltpu.VMEM((heads, rows, DV), F32),
            pltpu.VMEM((heads, WINDOW, DV), F32),
            pltpu.SemaphoreType.DMA((3,)),
            pltpu.SemaphoreType.DMA((2,)),
            pltpu.SemaphoreType.DMA((2,)),
            pltpu.SemaphoreType.DMA((heads, PIECES)),
            pltpu.SemaphoreType.DMA((heads, PIECES)),
        ],
        compiler_params=pltpu.CompilerParams(
            collective_id=0, has_side_effects=True, vmem_limit_bytes=48 * 2**20
        ),
    )(*[pltpu.with_memory_space_constraint(x, pltpu.HBM) for x in (queries, key_vectors, value_vectors)])


def solution(mesh):
    spec = P(("groups", "batch"), "seq", "head")
    return jax.shard_map(
        on_device, mesh=mesh, in_specs=(spec, spec, spec), out_specs=spec, check_vma=False
    )
```

```python
import jax
import jax.numpy as jnp
from jax import lax
from jax.experimental import pallas as pl
from jax.experimental.pallas import tpu as pltpu
from jax.sharding import PartitionSpec as P

DK = 16
DV = 128
WINDOW = 64
ROWS = 160
KEY_SUM_ROW = 137
PIECES = 1
LANES = 128
BLOCK = 256
SLOT = 32
BF16 = jnp.bfloat16
F32 = jnp.float32
MESH = pl.DeviceIdType.MESH


def iota(shape, dim):
    return lax.broadcasted_iota(jnp.int32, shape, dim)


def dot(a, b):
    return jnp.dot(a, b, preferred_element_type=F32)


def inverse(x):
    guess = pl.reciprocal(x, approx=True)
    return guess * (2.0 - x * guess)


def dot_nt(a, b):
    return lax.dot_general(a, b, (((1,), (1,)), ((), ())), preferred_element_type=F32)


def rolled_picker(distance, width):
    shape = (width, width)
    row, col = iota(shape, 0), iota(shape, 1)
    part = row & (DK - 1)
    target = row - part + ((part + distance) & (DK - 1))
    hit = target == col
    if distance == DK // 2:
        hit = hit & (part < DK // 2)
    return jnp.where(hit, 1.0 if distance == 0 else 0.25, 0.0).astype(BF16)


def pair_picker(heads):
    above = DK * (heads - 1)
    shape = (above + DK * heads, 2 * LANES)
    row, col = iota(shape, 0) - above, iota(shape, 1)
    part, turn = col & (DK - 1), (col & (LANES - 1)) >> 4
    right = col >= LANES
    hit = row == jnp.where(right, (part + turn) & (DK - 1), part)
    weight = jnp.where(right, jnp.where(turn == 0, 0.0625, 0.5), 1.0)
    return jnp.where(hit, weight, 0.0).astype(BF16)


def tail_picker(group, heads):
    shape = (DK * heads, 2 * LANES)
    row, col = iota(shape, 0), iota(shape, 1)
    slot, at = (col & (LANES - 1)) >> 5, col & (SLOT - 1)
    base = DK * (4 * group + slot)
    right = col >= LANES
    half = DK // 2
    left_hit = ((at < half) & (row == base + at)) | ((at >= DK) & (row == base + at - DK))
    right_hit = (at < half) & (row == base + at + half)
    picked = jnp.where(right, jnp.where(right_hit, 0.5, 0.0), jnp.where(left_hit, 1.0, 0.0))
    return picked.astype(BF16)


def kernel(
    n, heads,
    q_hbm, k_hbm, v_hbm, out_ref,
    q, kx, vx, phi_k, own, sent, prior, picker, tails, phi_q, sums, win, rim_win,
    load_sem, rim_send, rim_recv, send_sem, recv_sem,
):
    rows = q.shape[0]
    width = q.shape[1]
    groups = tails.shape[0]
    place = lax.axis_index("seq")
    has_prior = place > 0
    has_next = place < n - 1
    half = LANES // 2

    loads = [
        pltpu.make_async_copy(k_hbm.at[0], kx.at[pl.ds(LANES, rows)], load_sem.at[0]),
        pltpu.make_async_copy(v_hbm.at[0], vx.at[pl.ds(LANES, rows)], load_sem.at[1]),
        pltpu.make_async_copy(q_hbm.at[0], q, load_sem.at[2]),
    ]
    for load in loads:
        load.start()

    barrier = pltpu.get_barrier_semaphore()

    @pl.when(has_prior)
    def _():
        pl.semaphore_signal(barrier, inc=1, device_id={"seq": place - 1}, device_id_type=MESH)

    rim = [
        pltpu.make_async_remote_copy(
            src_ref=src.at[0, pl.ds(rows - WINDOW, WINDOW)],
            dst_ref=dst.at[pl.ds(half, WINDOW)],
            send_sem=rim_send.at[i],
            recv_sem=rim_recv.at[i],
            device_id={"seq": place + 1},
            device_id_type=MESH,
        )
        for i, (src, dst) in enumerate(((k_hbm, kx), (v_hbm, vx)))
    ]

    def chunk(h, piece):
        lines = pl.ds(piece * (ROWS // PIECES), ROWS // PIECES)
        return pltpu.make_async_remote_copy(
            src_ref=sent.at[h, lines],
            dst_ref=prior.at[h, lines],
            send_sem=send_sem.at[h, piece],
            recv_sem=recv_sem.at[h, piece],
            device_id={"seq": place + 1},
            device_id_type=MESH,
        )

    kx[0:half] = jnp.zeros((half, width), BF16)
    vx[0:half] = jnp.zeros((half, vx.shape[1]), BF16)

    @pl.when(jnp.logical_not(has_prior))
    def _():
        kx[half:LANES] = jnp.zeros((half, width), BF16)
        vx[half:LANES] = jnp.zeros((half, vx.shape[1]), BF16)
        prior[...] = jnp.zeros(prior.shape, BF16)

    loads[0].wait()

    keys = kx[LANES:LANES + rows]
    plain = dot_nt(rolled_picker(0, width), keys)

    def put(group, block):
        block = block.astype(BF16)
        for h in range(heads):
            phi_k[h, group * DK:(group + 1) * DK, :] = block[h * DK:(h + 1) * DK]

    put(0, plain * plain)
    for distance in range(1, DK // 2 + 1):
        other = dot_nt(rolled_picker(distance, width), keys)
        product = plain * other
        if distance == DK // 2:
            one = jnp.where(iota((width, 1), 0) & (DK - 1) == DK // 2, 1.0, 0.0)
            product = product + one
        put(distance, product)
    put(DK // 2 + 1, plain * 0.5)

    def with_ones(values):
        return jnp.concatenate([values, jnp.ones((values.shape[0], DV), BF16)], axis=1)

    @pl.when(has_next)
    def _():
        pl.semaphore_wait(barrier, 1)

    @pl.when(has_prior & has_next)
    def _():
        for copy in rim:
            copy.start()

    loads[1].wait()

    def state(h):
        full = dot(phi_k[h], with_ones(vx[LANES:LANES + rows, h * DV:(h + 1) * DV]))
        eye = iota((LANES, LANES), 0) == (iota((LANES, LANES), 1))
        key_sums = full[:, DV:]
        low = jnp.sum(jnp.where(eye, key_sums[:LANES], 0.0), axis=0, keepdims=True)
        hit = iota((SLOT, LANES), 0) == (iota((SLOT, LANES), 1) & (SLOT - 1))
        high = jnp.sum(jnp.where(hit, key_sums[LANES:], 0.0), axis=0, keepdims=True)
        row = iota((ROWS, DV), 0)
        own[h] = jnp.where(
            row == KEY_SUM_ROW, low, jnp.where(row == KEY_SUM_ROW + 1, high, full[:, :DV])
        )

    pair = 2 - heads % 2
    for first in range(0, heads, pair):
        for h in range(first, first + pair):
            state(h)

        @pl.when(jnp.logical_not(has_prior) & has_next)
        def _():
            for h in range(first, first + pair):
                sent[h] = own[h].astype(BF16)
                for piece in range(PIECES):
                    chunk(h, piece).start()

    picker[...] = pair_picker(heads)
    loads[2].wait()
    for group in range(groups):
        both = dot(q[...], tail_picker(group, heads))
        at = iota((1, LANES), 1) & (SLOT - 1)
        left = both[:, :LANES] + jnp.where(at == DK // 2, 2.0, 0.0)
        right = both[:, LANES:] + jnp.where((at == DK // 2) | (at >= DK), 1.0, 0.0)
        tails[group] = (left * right).astype(BF16)

    row = iota((LANES, LANES), 0)
    col = iota((LANES, LANES), 1)

    def head_scale(h):
        return jnp.where(iota((1, width), 1) >> 4 == h, 0.25, 0.0).astype(BF16)

    def lanes_of(h):
        return pl.ds(pl.multiple_of(h * DV, DV), DV)

    def local(members, big):
        near = (col <= row) & (row - col < WINDOW)
        far = (col > row + half)[:half]
        start = big * BLOCK
        until = start + BLOCK
        causal = iota((BLOCK, BLOCK), 1) <= iota((BLOCK, BLOCK), 0)
        scores = [
            dot_nt(q[start:until] * head_scale(h), kx[LANES:LANES + until]) for h in members
        ]
        chains = []
        for h, score in zip(members, scores):
            for small in range(BLOCK // LANES):
                begin = start + small * LANES
                part = score[small * LANES:(small + 1) * LANES]
                here = jnp.where(near, part[:, begin:begin + LANES], -jnp.inf)
                low = jnp.max(here[half:], axis=1, keepdims=True)
                if begin:
                    before = jnp.where(far, part[:half, begin - LANES:begin], -jnp.inf)
                    top = jnp.max(jnp.maximum(here[:half], before), axis=1, keepdims=True)
                    chains.append((h, begin, here, before, top, low))
                else:
                    chains.append((h, begin, here, None, None, low))
        for h, score in zip(members, scores):
            raised = score + 1.0
            weights = raised * raised + 1.0
            diagonal = jnp.where(causal, weights[:, start:], 0.0)
            if big:
                weights = jnp.concatenate([weights[:, :start], diagonal], axis=1)
            else:
                weights = diagonal
            sums[h, start:until] = dot(
                weights.astype(BF16), with_ones(vx[LANES:LANES + until, lanes_of(h)])
            )
        shares = []
        for h, begin, here, before, top, low in chains:
            if begin:
                share = jnp.concatenate(
                    [
                        jnp.concatenate(
                            [jnp.exp(before - top), jnp.zeros((half, LANES), F32)], axis=0
                        ),
                        jnp.exp(here - jnp.concatenate([top, low], axis=0)),
                    ],
                    axis=1,
                )
            else:
                share = jnp.exp(here[half:] - low)
            shares.append(share.astype(BF16))
        windows = []
        for (h, begin, *_), share in zip(chains, shares):
            first = begin if begin else LANES
            windows.append(
                dot(share, with_ones(vx[first:begin + 2 * LANES, lanes_of(h)]))
            )
        for h in members:
            pick = picker[pl.ds(pl.multiple_of(DK * (heads - 1 - h), DK), width)]
            both = dot(q[start:until], pick)
            phi_q[h, start:until] = (both[:, :LANES] * both[:, LANES:]).astype(BF16)
        for (h, begin, *_), both in zip(chains, windows):
            first = begin if begin else half
            win[h, first:begin + LANES] = both[:, :DV] * inverse(both[:, DV:])

    def edge():
        queries = jnp.concatenate([q[0:half] * head_scale(h) for h in range(heads)], axis=0)
        scores = dot_nt(queries, kx[0:2 * LANES])
        at = iota((half, 2 * LANES), 1)
        line = iota((half, 2 * LANES), 0)
        seen = (at > line + half) & (at <= line + LANES) & ((at >= LANES) | has_prior)
        shares = []
        for h in range(heads):
            score = jnp.where(seen, scores[h * half:(h + 1) * half], -jnp.inf)
            peak = jnp.max(
                jnp.maximum(score[:, :LANES], score[:, LANES:]), axis=1, keepdims=True
            )
            shares.append(jnp.exp(score - peak).astype(BF16))
        for h in range(heads):
            both = dot(shares[h], with_ones(vx[0:2 * LANES, h * DV:(h + 1) * DV]))
            rim_win[h] = both[:, :DV] * inverse(both[:, DV:])

    def forward(first, end):
        def one(h, carry):
            for piece in range(PIECES):
                chunk(h, piece).wait_recv()
                lines = slice(piece * (ROWS // PIECES), (piece + 1) * (ROWS // PIECES))

                @pl.when(has_next)
                def _():
                    sent[h, lines] = (prior[h, lines].astype(F32) + own[h, lines]).astype(BF16)
                    chunk(h, piece).start()

            return carry

        @pl.when(has_prior)
        def _():
            lax.fori_loop(first, end, one, 0)

    def finish(members):
        totals = []
        for h in members:
            before = prior[h]
            wide = before[DK * 8:DK * 9].astype(F32)
            at = KEY_SUM_ROW - DK * 8
            lane = iota((1, LANES), 1)
            high = jnp.where(lane >> 5 == (h & 3), wide[at + 1:at + 2], 0.0)
            key_sums = jnp.concatenate([wide[at:at + 1], high], axis=1).astype(BF16)
            key_sums = jnp.broadcast_to(key_sums, (DV, 2 * LANES))
            tail = jnp.concatenate([before[LANES:]] * (LANES // SLOT), axis=0)
            slot = iota((LANES, 1), 0) >> 5
            tail = jnp.where(slot == (h & 3), tail, jnp.zeros_like(tail))
            state = jnp.concatenate([before[:LANES], tail], axis=0)
            feats = jnp.concatenate([phi_q[h], tails[h >> 2]], axis=1)
            totals.append((dot(feats, state), dot_nt(feats, key_sums)))
        for h, (total, weight) in zip(members, totals):
            total = sums[h, :, :DV] + total
            weight = sums[h, :, DV:] + weight
            linear = total * inverse(weight)
            win[h, 0:half] = linear[0:half]
            out_ref[0, half:rows, lanes_of(h)] = (win[h, half:rows] + linear[half:]).astype(BF16)

    blocks = rows // BLOCK
    steps = heads // pair
    units = blocks * steps
    delay = jnp.where(has_next, 10 + 10 * jnp.maximum(place - 1, 0), 1000)

    def due(unit):
        return jnp.minimum(jnp.maximum(6 * (unit + 1) - delay, 0) // 4, heads)

    def needed(t):
        return jnp.maximum(pair * t, due(units + t))

    def spread(t, carry):
        members = [pair * t + e for e in range(pair)]
        for order in range(blocks):
            local(members, blocks - 1 - order)
            unit = blocks * t + order
            forward(due(unit - 1), due(unit))
        return carry

    lax.fori_loop(0, steps, spread, 0)
    forward(due(units - 1), due(units))

    @pl.when(jnp.logical_not(has_prior) & has_next)
    def _():
        for copy in rim:
            copy.start()

    rim_late = place == 1

    @pl.when(has_prior & jnp.logical_not(rim_late))
    def _():
        for copy in rim:
            copy.wait_recv()

    @pl.when(jnp.logical_not(rim_late))
    def _():
        edge()

    def gather(t, carry):
        members = [pair * t + e for e in range(pair)]
        forward(needed(t), needed(t + 1))
        finish(members)
        return carry

    lax.fori_loop(0, steps, gather, 0)

    @pl.when(rim_late)
    def _():
        for copy in rim:
            copy.wait_recv()
        edge()

    for h in range(heads):
        out_ref[0, 0:half, h * DV:(h + 1) * DV] = (rim_win[h] + win[h, 0:half]).astype(BF16)

    @pl.when(has_next)
    def _():
        for copy in rim:
            copy.wait_send()

        def drain(h, carry):
            for piece in range(PIECES):
                chunk(h, piece).wait_send()
            return carry

        lax.fori_loop(0, heads, drain, 0)


def on_device(queries, key_vectors, value_vectors):
    n = lax.axis_size("seq")
    rows, width = queries.shape[1:]
    heads = width // DK
    values = value_vectors.shape[2]
    groups = -(-heads // 4)
    any_space = pl.BlockSpec(memory_space=pl.ANY)

    def body(*refs):
        kernel(n, heads, *refs)

    return pl.pallas_call(
        body,
        out_shape=jax.ShapeDtypeStruct((1, rows, values), BF16),
        in_specs=[any_space] * 3,
        out_specs=pl.BlockSpec(memory_space=pltpu.VMEM),
        scratch_shapes=[
            pltpu.VMEM((rows, width), BF16),
            pltpu.VMEM((LANES + rows, width), BF16),
            pltpu.VMEM((LANES + rows, values), BF16),
            pltpu.VMEM((heads, ROWS, rows), BF16),
            pltpu.VMEM((heads, ROWS, DV), F32),
            pltpu.VMEM((heads, ROWS, DV), BF16),
            pltpu.VMEM((heads, ROWS, DV), BF16),
            pltpu.VMEM((DK * (2 * heads - 1), 2 * LANES), BF16),
            pltpu.VMEM((groups, rows, LANES), BF16),
            pltpu.VMEM((heads, rows, LANES), BF16),
            pltpu.VMEM((heads, rows, 2 * DV), F32),
            pltpu.VMEM((heads, rows, DV), F32),
            pltpu.VMEM((heads, WINDOW, DV), F32),
            pltpu.SemaphoreType.DMA((3,)),
            pltpu.SemaphoreType.DMA((2,)),
            pltpu.SemaphoreType.DMA((2,)),
            pltpu.SemaphoreType.DMA((heads, PIECES)),
            pltpu.SemaphoreType.DMA((heads, PIECES)),
        ],
        compiler_params=pltpu.CompilerParams(
            collective_id=0, has_side_effects=True, vmem_limit_bytes=48 * 2**20
        ),
    )(*[pltpu.with_memory_space_constraint(x, pltpu.HBM) for x in (queries, key_vectors, value_vectors)])


def solution(mesh):
    spec = P(("groups", "batch"), "seq", "head")
    return jax.shard_map(
        on_device, mesh=mesh, in_specs=(spec, spec, spec), out_specs=spec, check_vma=False
    )
```
